256 devices in a mesh: blk: 32 (over z, y_hi, core), rep: 8 (over x, y_lo).
Axes of the slice: x: 4, y: 4 (y_hi: 2, y_lo: 2; y = y_hi * 2 + y_lo), z: 8, core: 2. Of those that a mesh axis runs over, the one named last changes fastest.
Arguments:
- embeddings: float32 [32768, 768], P(('blk', 'rep')), may hold values from -48 to 48
- labels: float32 [32768, 128], P(('blk', 'rep')), may hold values from -6 to 6
Outputs:
- updated: float32 [32768, 128], P(('blk', 'rep'))
The draws below stay inside these ranges and needn't reach their ends.
All inputs are finite; a program needn't handle non-finite values.
Results may differ from the reference program's by a relative error of at most 0.0003.
Values sent between devices are 32-bit elements; how exact they have to be, the bound alone decides.
A program may use at most 64 MiB of HBM per device.

```python
import math
import jax
import jax.numpy as jnp
from jax import lax

EMBED = 768
LABELS = 128
ROWS_DEV = 128
POINTS = 32768
N_BLK = 32
N_REP = 8


def draw_embeddings(key, part):
    key = jax.random.fold_in(key, 11)
    keys = jax.random.split(key, 8)
    base = jnp.clip(jax.random.normal(keys[0], (POINTS, EMBED), jnp.float32), -4.0, 4.0)
    row_scale = jnp.exp(jax.random.uniform(keys[2], (POINTS, 1), jnp.float32, math.log(0.25), math.log(2.5)))
    col_scale = jnp.exp(jax.random.uniform(keys[3], (1, EMBED), jnp.float32, math.log(0.5), math.log(2.0)))
    strong = 2.5
    position = jnp.arange(POINTS, dtype=jnp.int32)[:, None] % 97
    anchor_scale = strong * jnp.exp(jax.random.uniform(keys[4], (POINTS, 1), jnp.float32, math.log(0.84), 0.0))
    noise = 0.02 * jax.random.normal(keys[5], (POINTS, EMBED), jnp.float32)
    first_copy = jnp.roll(base, 1, axis=0) + noise
    second_copy = 1.012 * jnp.roll(base, 2, axis=0) + noise
    base = jnp.where(position == 1, first_copy, jnp.where(position == 2, second_copy, base))
    scale_one = jnp.roll(anchor_scale, 1, axis=0)
    scale_two = jnp.roll(anchor_scale, 2, axis=0)
    row_scale = jnp.where(position == 0, anchor_scale, jnp.where(position == 1, scale_one, jnp.where(position == 2, scale_two, row_scale)))
    group = jax.random.randint(keys[6], (POINTS,), 0, 16)
    directions = jnp.clip(jax.random.normal(keys[7], (16, EMBED), jnp.float32), -3.0, 3.0)
    shared = jnp.take(directions, group, axis=0)
    base = jnp.where(row_scale < 0.7, base + shared, base)
    return (row_scale * col_scale * base).astype(jnp.float32)


def levels(rng, dims, cuts, low, high):
    level = 1.0
    for dim, parts in cuts:
        draws = jax.random.uniform(jax.random.fold_in(jax.random.fold_in(rng, 6), dim), (parts,), jnp.float32, low / len(cuts), high / len(cuts))
        level = level * jnp.repeat(jnp.exp(draws), dims[dim] // parts).reshape((-1,) + (1,) * (len(dims) - 1 - dim))
    return level


def centred(stream_key, dims, spread, reach, cuts=(), kind=jnp.bfloat16):
    array = jax.random.normal(stream_key, dims, jnp.float32) * spread
    if len(cuts) > 0:
        array = levels(stream_key, dims, cuts, -0.22, 0.18) * array
    return jnp.clip(array, min=-reach, max=reach).astype(kind)


def setup_inputs(seed: int = 0) -> dict:
    arg_keys = jax.random.split(jax.random.key(seed), 3)
    return {
        "embeddings": draw_embeddings(jax.random.fold_in(arg_keys[2], 71), 0),
        "labels": centred(arg_keys[1], (POINTS, LABELS), 1.0, 6.0, ((0, 256),), jnp.float32),
    }


def reference(embeddings, labels):
    point_count = embeddings.shape[0]
    slab_rows = ROWS_DEV * N_REP
    factor = 1.0 / math.sqrt(EMBED)
    columns = jnp.arange(point_count, dtype=jnp.int32)

    def one_slab(start):
        queries = lax.dynamic_slice_in_dim(embeddings, start, slab_rows, 0)
        scores = jnp.dot(queries, embeddings.T, precision=lax.Precision.HIGHEST, preferred_element_type=jnp.float32) * factor
        row_ids = start + jnp.arange(slab_rows, dtype=jnp.int32)
        scores = jnp.where(row_ids[:, None] == columns[None, :], -jnp.inf, scores)
        top_score = lax.optimization_barrier(jnp.max(scores, axis=1, keepdims=True))
        weights = jnp.exp(scores - top_score)
        total = lax.optimization_barrier(jnp.sum(weights, axis=1, keepdims=True))
        weighted = jnp.dot(weights, labels, precision=lax.Precision.HIGHEST, preferred_element_type=jnp.float32)
        return weighted / total
    starts = jnp.arange(N_BLK, dtype=jnp.int32) * slab_rows
    propagated = lax.map(one_slab, starts).reshape(point_count, labels.shape[1])
    return 0.1 * labels + 0.9 * propagated
```

```python
import math

import jax
import jax.numpy as jnp
from jax import lax
from jax.experimental import pallas as pl
from jax.experimental.pallas import tpu as pltpu
from jax.sharding import PartitionSpec as P

MESH = pl.DeviceIdType.MESH
F32, BF16 = jnp.float32, jnp.bfloat16
ROWS, DIM, LAB = 128, 768, 128
GQ, UK = 512, 256
NG, NU = 4, 8
NEG = -1e30
NT = (((1,), (1,)), ((), ()))
NN = (((1,), (0,)), ((), ()))

BLOCKS = [
    (1, 0), (3, 0), (0, 1), (0, 3),
    (1, 1), (1, 3), (3, 1), (3, 3),
    (0, 0), (2, 0), (0, 2), (1, 2),
    (3, 2), (2, 1), (2, 3), (2, 2),
]
SLOT = {block: i for i, block in enumerate(BLOCKS)}
OWN = SLOT[(0, 0)]
LINKS = [("x", 1), ("x", -1), ("y", 1), ("y", -1)]

ORDER = [('kc', 0), ('q', 0), ('z', 1), ('kc', 1), ('q', 1), ('qc', 0), ('t', 0, 0), ('z', 2), ('t', 0, 1), ('q', 2), ('kc', 2), ('t', 0, 2), ('q', 3), ('z', 3), ('q', 4), ('kc', 3), ('t', 0, 3), ('z', 4), ('q', 5), ('qc', 1), ('t', 1, 0), ('kc', 4), ('t', 1, 1), ('t', 1, 2), ('z', 5), ('t', 1, 3), ('q', 6), ('t', 0, 4), ('t', 1, 4), ('kc', 5), ('q', 7), ('qc', 2), ('t', 2, 0), ('t', 2, 1), ('z', 6), ('q', 8), ('t', 2, 2), ('t', 2, 3), ('q', 9), ('kc', 6), ('qc', 3), ('t', 3, 0), ('t', 3, 1), ('z', 7), ('t', 3, 2), ('t', 3, 3), ('t', 2, 4), ('kc', 7), ('t', 3, 4), ('t', 3, 5), ('t', 3, 6), ('t', 3, 7), ('f', 3), ('t', 1, 5), ('t', 1, 6), ('t', 1, 7), ('f', 1), ('t', 0, 5), ('t', 0, 6), ('t', 0, 7), ('f', 0), ('t', 2, 5), ('t', 2, 6), ('t', 2, 7), ('f', 2)]


def split_order(order):
    tiles, before, after, waiting = [], [], {}, []
    for item in order:
        if item[0] == "t":
            tiles.append((item[1], item[2]))
            before.append(waiting)
            waiting = []
        elif item[0] == "f":
            after[len(tiles) - 1] = item[1]
        else:
            waiting.append(item)
    return tiles, before, after


def pick(i, values):
    out = jnp.int32(values[0])
    for j in range(1, len(values)):
        if values[j] != values[j - 1]:
            out = jnp.where(i >= j, jnp.int32(values[j]), out)
    return out


def device(x, y, z, c):
    return ((z * 2 + y // 2) * 2 + c, x * 2 + lax.rem(y, 2))


def kernel(emb, lab, out, qf, kf, qh, ql, kh, kl, vt, s_buf, acc, m_ref, l_ref, back,
           q_send, q_recv, z_send, z_recv, d_send, d_recv, b_send, b_recv):
    blk, rep = lax.axis_index("blk"), lax.axis_index("rep")
    mx, my = rep // 2, lax.rem(blk // 2, 2) * 2 + lax.rem(rep, 2)
    mz, mc = blk // 4, lax.rem(blk, 2)

    def at(dx=0, dy=0, dz=0, dc=0):
        return device(lax.rem(mx + dx % 4, 4), lax.rem(my + dy % 4, 4), lax.rem(mz + dz % 8, 8), lax.rem(mc + dc, 2))

    barrier = pltpu.get_barrier_semaphore()
    peers = [at(dx=b[0], dy=b[1]) for b in BLOCKS if b != (0, 0)] + [at(dz=1), at(dz=-1), at(dc=1)]
    for peer in peers:
        pl.semaphore_signal(barrier, inc=1, device_id=peer, device_id_type=MESH)
    kf[0, :ROWS, :DIM] = emb[...]
    kf[0, :ROWS, DIM:] = lab[...]
    qf[OWN] = emb[...]
    m_ref[...] = jnp.full_like(m_ref, NEG)
    l_ref[...] = jnp.zeros_like(l_ref)
    acc[...] = jnp.zeros_like(acc)
    pl.semaphore_wait(barrier, len(peers))

    def remote(src, dst, send, recv, to):
        return pltpu.make_async_remote_copy(
            src_ref=src, dst_ref=dst, send_sem=send, recv_sem=recv, device_id=to, device_id_type=MESH
        )

    def plane(link, n):
        axis, sign = LINKS[link]
        near, far = ((0, 64), (64, 64)) if axis == "x" else ((64, 64), (0, 64))
        half = 0 if sign == 1 else 32
        near_part, far_part = (near[0] + half, 32), (far[0] + half, 32)
        along, across, part = [
            (0, 0, near), (0, 0, far), (-sign, 0, near_part), (-sign, 0, far_part),
            (0, 1, far), (0, -1, far), (0, 2, far),
            (-sign, 1, far_part), (-sign, -1, far_part), (-sign, 2, far_part),
        ][n]
        here, there = (along, across), (along - sign, across)
        step = (sign, 0)
        if axis == "y":
            here, there, step = here[::-1], there[::-1], step[::-1]
        mine = SLOT[(here[0] % 4, here[1] % 4)]
        theirs = SLOT[(there[0] % 4, there[1] % 4)]
        rows = pl.ds(part[0], part[1])
        return remote(qf.at[mine, rows], qf.at[theirs, rows], q_send.at[link, n], q_recv.at[link, n],
                      at(dx=step[0], dy=step[1]))

    def ring(way, r):
        sign = 1 if way == 0 else -1
        theirs = pl.ds(64 * way, 64)
        if r == 1:
            src = kf.at[0, pl.ds(64 * way, 64)]
        elif r == 2:
            src = kf.at[0, pl.ds(64 - 64 * way, 64)]
        else:
            src = kf.at[r - 2, theirs]
        return remote(src, kf.at[r, theirs], z_send.at[way, r], z_recv.at[way, r], at(dz=sign))

    def across(u):
        return remote(kf.at[u, pl.ds(0, ROWS)], kf.at[u, pl.ds(ROWS, ROWS)], d_send.at[u], d_recv.at[u], at(dc=1))

    def home(slot):
        dx, dy = BLOCKS[slot]
        return remote(acc.at[slot], back.at[slot], b_send.at[slot], b_recv.at[slot], at(dx=dx, dy=dy))

    for n in range(2):
        for link in range(4):
            plane(link, n).start()
        for way in range(2):
            ring(way, n + 1).start()
    across(0).start()

    scale = math.log2(math.e) / math.sqrt(DIM)

    def convert_queries(g):
        for b in range(4):
            slot = 4 * g + b

            def chunk(i, carry, slot=slot):
                rows = pl.ds(pl.multiple_of(i * 32, 32), 32)
                value = qf[slot, rows, :] * scale
                high = value.astype(BF16)
                to = pl.ds(pl.multiple_of(slot * ROWS + i * 32, 32), 32)
                qh[to, :] = high
                ql[to, :] = (value - high.astype(F32)).astype(BF16)
                return carry

            lax.fori_loop(0, ROWS // 32, chunk, 0)

    def convert_keys(u):
        def chunk(i, carry):
            rows = pl.ds(pl.multiple_of(i * 32, 32), 32)
            value = kf[u, rows, :DIM]
            high = value.astype(BF16)
            to = pl.ds(pl.multiple_of(u * UK + i * 32, 32), 32)
            kh[to, :] = high
            kl[to, :] = (value - high.astype(F32)).astype(BF16)
            return carry

        lax.fori_loop(0, UK // 32, chunk, 0)
        value = kf[u, :, DIM:].T
        high = value.astype(BF16)
        vt[:LAB, u * UK:(u + 1) * UK] = high
        vt[LAB:, u * UK:(u + 1) * UK] = (value - high.astype(F32)).astype(BF16)

    def event(item):
        kind, n = item
        if kind == "q":
            for link in range(4):
                plane(link, n).wait_recv()
            if n + 2 < 10:
                for link in range(4):
                    plane(link, n + 2).start()
        elif kind == "z":
            for way in range(2):
                ring(way, n).wait_recv()
                if n + 2 < NU:
                    ring(way, n + 2).start()
            across(n).start()
        elif kind == "kc":
            across(n).wait_recv()
            convert_keys(n)
        else:
            convert_queries(n)

    def finish(g):
        for b in range(4):
            slot = 4 * g + b
            acc[slot, LAB:LAB + 1, :] = m_ref[g, :, b * ROWS:(b + 1) * ROWS]
            acc[slot, LAB + 1:LAB + 2, :] = l_ref[g, :, b * ROWS:(b + 1) * ROWS]
            if slot != OWN:
                home(slot).start()

    def scores(g, u):
        queries = pl.ds(pl.multiple_of(g * GQ, GQ), GQ)
        keys = pl.ds(pl.multiple_of(u * UK, UK), UK)
        a, b = kh[keys, :], qh[queries, :]
        s = lax.dot_general(a, b, NT, preferred_element_type=F32)
        s += lax.dot_general(kl[keys, :], b, NT, preferred_element_type=F32)
        s += lax.dot_general(a, ql[queries, :], NT, preferred_element_type=F32)
        return s

    def absorb(g, u, s):
        keys = pl.ds(pl.multiple_of(u * UK, UK), UK)
        m_old = m_ref[g]
        m_new = jnp.maximum(m_old, jnp.max(s, axis=0, keepdims=True))
        shrink = jnp.exp2(m_old - m_new)
        p = jnp.exp2(s - m_new)
        m_ref[g] = m_new
        l_ref[g] = l_ref[g] * shrink + jnp.sum(p, axis=0, keepdims=True)
        high = p.astype(BF16)
        low = (p - high.astype(F32)).astype(BF16)
        v = vt[:, keys]
        o = lax.dot_general(v, high, NN, preferred_element_type=F32)
        o = o[:LAB] + o[LAB:] + lax.dot_general(v[:LAB], low, NN, preferred_element_type=F32)
        for b in range(4):
            cols = slice(b * ROWS, (b + 1) * ROWS)
            acc[g * 4 + b, :LAB, :] = acc[g * 4 + b, :LAB, :] * shrink[:, cols] + o[:, cols]

    def exclude_self(g, u, slot):
        @pl.when((g == OWN // 4) & (u == 0))
        def _():
            block = s_buf[slot, :ROWS, (OWN % 4) * ROWS:(OWN % 4 + 1) * ROWS]
            same = lax.broadcasted_iota(jnp.int32, block.shape, 0) == lax.broadcasted_iota(jnp.int32, block.shape, 1)
            s_buf[slot, :ROWS, (OWN % 4) * ROWS:(OWN % 4 + 1) * ROWS] = jnp.where(same, NEG, block)

    tiles, before, after = split_order(ORDER)
    groups, units = [t[0] for t in tiles], [t[1] for t in tiles]
    count = len(tiles)

    def when_step(j, parity, table, act):
        for step in range(parity, count - 2, 2):
            if table(step):
                @pl.when(j == step)
                def _(step=step):
                    act(step)

    def act_before(step):
        for item in before[step + 1]:
            event(item)

    for item in before[0]:
        event(item)
    s_buf[0] = scores(groups[0], units[0])
    exclude_self(groups[0], units[0], 0)

    def body(i, carry):
        for parity in range(2):
            j = 2 * i + parity
            when_step(j, parity, lambda step: before[step + 1], act_before)
            g, u = pick(j, groups), pick(j, units)
            g_next, u_next = pick(j + 1, groups), pick(j + 1, units)
            following = scores(g_next, u_next)
            absorb(g, u, s_buf[parity])
            s_buf[1 - parity] = following
            exclude_self(g_next, u_next, 1 - parity)
            when_step(j, parity, lambda step: step in after, lambda step: finish(after[step]))
        return carry

    lax.fori_loop(0, (count - 2) // 2, body, 0)
    for item in before[count - 1]:
        event(item)
    following = scores(groups[-1], units[-1])
    absorb(groups[-2], units[-2], s_buf[0])
    s_buf[1] = following
    if count - 2 in after:
        finish(after[count - 2])
    absorb(groups[-1], units[-1], s_buf[1])
    finish(after[count - 1])

    others = [s for s in range(len(BLOCKS)) if s != OWN]
    for slot in others:
        home(slot).wait_recv()
    top = acc[OWN, LAB:LAB + 1, :]
    for slot in others:
        top = jnp.maximum(top, back[slot, LAB:LAB + 1, :])
    total = jnp.zeros_like(top)
    summed = jnp.zeros((LAB, ROWS), F32)
    for slot in range(len(BLOCKS)):
        ref = acc if slot == OWN else back
        weight = jnp.exp2(ref[slot, LAB:LAB + 1, :] - top)
        total += weight * ref[slot, LAB + 1:LAB + 2, :]
        summed += weight * ref[slot, :LAB, :]
    out[...] = 0.1 * lab[...] + 0.9 * (summed / total).T

    for n in range(10):
        for link in range(4):
            plane(link, n).wait_send()
    for r in range(1, NU):
        for way in range(2):
            ring(way, r).wait_send()
    for u in range(NU):
        across(u).wait_send()
    for slot in others:
        home(slot).wait_send()


def body(embeddings, labels):
    vmem = pl.BlockSpec(memory_space=pltpu.VMEM)
    return pl.pallas_call(
        kernel,
        out_shape=jax.ShapeDtypeStruct((ROWS, LAB), F32),
        in_specs=[vmem, vmem],
        out_specs=vmem,
        scratch_shapes=[
            pltpu.VMEM((16, ROWS, DIM), F32),
            pltpu.VMEM((NU, UK, DIM + LAB), F32),
            pltpu.VMEM((NG * GQ, DIM), BF16),
            pltpu.VMEM((NG * GQ, DIM), BF16),
            pltpu.VMEM((NU * UK, DIM), BF16),
            pltpu.VMEM((NU * UK, DIM), BF16),
            pltpu.VMEM((2 * LAB, NU * UK), BF16),
            pltpu.VMEM((2, UK, GQ), F32),
            pltpu.VMEM((16, LAB + 8, ROWS), F32),
            pltpu.VMEM((NG, 1, GQ), F32),
            pltpu.VMEM((NG, 1, GQ), F32),
            pltpu.VMEM((16, LAB + 8, ROWS), F32),
            pltpu.SemaphoreType.DMA((4, 10)),
            pltpu.SemaphoreType.DMA((4, 10)),
            pltpu.SemaphoreType.DMA((2, NU)),
            pltpu.SemaphoreType.DMA((2, NU)),
            pltpu.SemaphoreType.DMA((NU,)),
            pltpu.SemaphoreType.DMA((NU,)),
            pltpu.SemaphoreType.DMA((16,)),
            pltpu.SemaphoreType.DMA((16,)),
        ],
        compiler_params=pltpu.CompilerParams(
            collective_id=0, has_side_effects=True, vmem_limit_bytes=56 * 2**20
        ),
        name="propagate",
    )(embeddings, labels)


def solution(mesh):
    placed = P(("blk", "rep"), None)
    return jax.shard_map(body, mesh=mesh, in_specs=(placed, placed), out_specs=placed, check_vma=False)
```

```python
import math

import jax
import jax.numpy as jnp
from jax import lax
from jax.experimental import pallas as pl
from jax.experimental.pallas import tpu as pltpu
from jax.sharding import PartitionSpec as P

MESH = pl.DeviceIdType.MESH
F32, BF16 = jnp.float32, jnp.bfloat16
ROWS, DIM, LAB = 128, 768, 128
GQ, UK = 512, 512
NG, NU = 4, 4
RING, NR = 256, 8
NEG = -1e30
NT = (((1,), (1,)), ((), ()))
NN = (((1,), (0,)), ((), ()))

HALVES = [
    (1, 0, 0), (1, 0, 1), (3, 0, 0), (3, 0, 1), (0, 1, 0), (0, 1, 1), (0, 3, 0), (0, 3, 1),
    (0, 0, 0), (0, 0, 1), (2, 0, 0), (2, 0, 1), (0, 2, 0), (0, 2, 1), (1, 1, 0), (1, 1, 1),
    (3, 3, 0), (3, 3, 1), (1, 3, 0), (1, 3, 1), (3, 1, 0), (3, 1, 1), (2, 1, 0), (1, 2, 1),
    (1, 2, 0), (2, 1, 1), (3, 2, 0), (3, 2, 1), (2, 3, 0), (2, 3, 1), (2, 2, 0), (2, 2, 1),
]
BLOCKS = sorted({half[:2] for half in HALVES})
SLOT = {block: i for i, block in enumerate(BLOCKS)}
OWN = SLOT[(0, 0)]
OWN_GROUP, OWN_COL = HALVES.index((0, 0, 0)) // 8, HALVES.index((0, 0, 0)) % 8 * 64
FIRST = {(1, 1): (0, 1), (3, 3): (0, 3), (1, 3): (1, 0), (3, 1): (3, 0), (1, 2): (0, 2), (3, 2): (0, 2), (2, 1): (2, 0), (2, 3): (2, 0)}
ADDED = {(1, 0): [(1, 1), (1, 2)], (3, 0): [(3, 3), (3, 2)], (0, 1): [(3, 1), (2, 1)], (0, 3): [(1, 3), (2, 3)]}
DIRECT = [(2, 0), (0, 2), (2, 2)]
LINKS = [("x", 1), ("x", -1), ("y", 1), ("y", -1)]

ORDER = [
    ("kc", 0), ("q", 0), ("z", 1), ("kc", 1), ("q", 1), ("qc", 0), ("t", 0, 0), ("z", 2), ("q", 2), ("kc", 2),
    ("q", 3), ("z", 3), ("q", 4), ("qc", 1), ("kc", 3), ("t", 1, 0), ("t", 0, 1), ("z", 4), ("t", 1, 1), ("q", 5),
    ("kc", 4), ("q", 6), ("qc", 2), ("z", 5), ("t", 2, 0), ("kc", 5), ("q", 7), ("t", 2, 1), ("t", 0, 2), ("q", 8),
    ("z", 6), ("t", 1, 2), ("q", 9), ("kc", 6), ("qc", 3), ("t", 3, 0), ("t", 3, 1), ("z", 7), ("t", 3, 2),
    ("kc", 7), ("t", 3, 3), ("f", 3), ("t", 1, 3), ("f", 1), ("t", 2, 2), ("t", 2, 3), ("f", 2), ("t", 0, 3),
    ("f", 0),
]


def split_order(order):
    tiles, before, after, waiting = [], [], {}, []
    for item in order:
        if item[0] == "t":
            tiles.append((item[1], item[2]))
            before.append(waiting)
            waiting = []
        elif item[0] == "f":
            after[len(tiles) - 1] = item[1]
        else:
            waiting.append(item)
    return tiles, before, after


def pick(i, values):
    out = jnp.int32(values[0])
    for j in range(1, len(values)):
        if values[j] != values[j - 1]:
            out = jnp.where(i >= j, jnp.int32(values[j]), out)
    return out


def device(x, y, z, c):
    return ((z * 2 + y // 2) * 2 + c, x * 2 + lax.rem(y, 2))


def kernel(emb, lab, out, qf, kf, qh, ql, kh, kl, vt, s_buf, acc, m_ref, l_ref, state, back,
           in_sem, q_send, q_recv, z_send, z_recv, d_send, d_recv, b_send, b_recv):
    blk, rep = lax.axis_index("blk"), lax.axis_index("rep")
    mx, my = rep // 2, lax.rem(blk // 2, 2) * 2 + lax.rem(rep, 2)
    mz, mc = blk // 4, lax.rem(blk, 2)

    def at(dx=0, dy=0, dz=0, dc=0):
        return device(lax.rem(mx + dx % 4, 4), lax.rem(my + dy % 4, 4), lax.rem(mz + dz % 8, 8), lax.rem(mc + dc, 2))

    barrier = pltpu.get_barrier_semaphore()
    peers = [at(dx=b[0], dy=b[1]) for b in [*ADDED, *DIRECT]] + [at(dz=1), at(dz=-1), at(dc=1)]
    for peer in peers:
        pl.semaphore_signal(barrier, inc=1, device_id=peer, device_id_type=MESH)
    own = [
        pltpu.make_async_copy(emb, kf.at[0, pl.ds(0, ROWS), pl.ds(0, DIM)], in_sem.at[0]),
        pltpu.make_async_copy(lab, kf.at[0, pl.ds(0, ROWS), pl.ds(DIM, LAB)], in_sem.at[1]),
    ]
    for copy in own:
        copy.start()
    m_ref[...] = jnp.full_like(m_ref, NEG)
    l_ref[...] = jnp.zeros_like(l_ref)
    acc[...] = jnp.zeros_like(acc)
    for copy in own:
        copy.wait()
    qf[OWN] = kf[0, :ROWS, :DIM] * (math.log2(math.e) / math.sqrt(DIM))
    pl.semaphore_wait(barrier, len(peers))

    def remote(src, dst, send, recv, to):
        return pltpu.make_async_remote_copy(
            src_ref=src, dst_ref=dst, send_sem=send, recv_sem=recv, device_id=to, device_id_type=MESH
        )

    def plane(link, n):
        axis, sign = LINKS[link]
        near, far = ((0, 64), (64, 64)) if axis == "x" else ((64, 64), (0, 64))
        half = 0 if sign == 1 else 32
        near_part, far_part = (near[0] + half, 32), (far[0] + half, 32)
        along, across, part = [
            (0, 0, near), (0, 0, far), (-sign, 0, near_part), (-sign, 0, far_part),
            (0, 1, far), (0, -1, far), (0, 2, far),
            (-sign, 1, far_part), (-sign, -1, far_part), (-sign, 2, far_part),
        ][n]
        here, there = (along, across), (along - sign, across)
        step = (sign, 0)
        if axis == "y":
            here, there, step = here[::-1], there[::-1], step[::-1]
        mine = SLOT[(here[0] % 4, here[1] % 4)]
        theirs = SLOT[(there[0] % 4, there[1] % 4)]
        rows = pl.ds(part[0], part[1])
        return remote(qf.at[mine, rows], qf.at[theirs, rows], q_send.at[link, n], q_recv.at[link, n],
                      at(dx=step[0], dy=step[1]))

    def ring(way, r):
        sign = 1 if way == 0 else -1
        theirs = pl.ds(64 * way, 64)
        if r == 1:
            src = kf.at[0, pl.ds(64 * way, 64)]
        elif r == 2:
            src = kf.at[0, pl.ds(64 - 64 * way, 64)]
        else:
            src = kf.at[r - 2, theirs]
        return remote(src, kf.at[r, theirs], z_send.at[way, r], z_recv.at[way, r], at(dz=sign))

    def across(way, r):
        return remote(kf.at[r, pl.ds(64 * way, 64)], kf.at[r, pl.ds(ROWS + 64 * way, 64)],
                      d_send.at[way, r], d_recv.at[way, r], at(dc=1))

    def home(slot):
        dx, dy = FIRST.get(BLOCKS[slot], BLOCKS[slot])
        return remote(state.at[slot], back.at[slot], b_send.at[slot], b_recv.at[slot], at(dx=dx, dy=dy))

    for n in range(2):
        for link in range(4):
            plane(link, n).start()
        for way in range(2):
            ring(way, n + 1).start()
    for way in range(2):
        across(way, 0).start()

    def halves(value):
        high = value.astype(BF16)
        return high, (value - high.astype(F32)).astype(BF16)

    def convert_queries(g):
        for i in range(8 * g, 8 * g + 8):
            dx, dy, half = HALVES[i]
            rows = pl.ds(i * 64, 64)
            qh[rows, :], ql[rows, :] = halves(qf[SLOT[(dx, dy)], half * 64:half * 64 + 64])

    def convert_keys(r):
        for start in range(0, RING, ROWS):
            rows = pl.ds(r * RING + start, ROWS)
            kh[rows, :], kl[rows, :] = halves(kf[r, start:start + ROWS, :DIM])
        cols = pl.ds(r * RING, RING)
        vt[:LAB, cols], vt[LAB:, cols] = halves(kf[r, :, DIM:].T)

    def event(item):
        kind, n = item
        if kind == "q":
            for link in range(4):
                plane(link, n).wait_recv()
            if n + 2 < 10:
                for link in range(4):
                    plane(link, n + 2).start()
        elif kind == "z":
            for way in range(2):
                ring(way, n).wait_recv()
                if n + 2 < NR:
                    ring(way, n + 2).start()
                across(way, n).start()
        elif kind == "kc":
            for way in range(2):
                across(way, n).wait_recv()
            convert_keys(n)
        else:
            convert_queries(n)

    def finish(g):
        for pair in range(4):
            first, second = (SLOT[HALVES[8 * g + 2 * pair + h][:2]] for h in range(2))
            cols = slice(pair * ROWS, (pair + 1) * ROWS)
            for rows, value in (
                (slice(0, LAB), acc[g, :, cols]),
                (slice(LAB, LAB + 1), m_ref[g, :, cols]),
                (slice(LAB + 1, LAB + 2), l_ref[g, :, cols]),
            ):
                if first == second:
                    state[first, rows, :] = value
                else:
                    state[first, rows, :64] = value[:, :64]
                    state[second, rows, 64:] = value[:, 64:]
        for slot in complete[g]:
            home(slot).start()

    def scores(g, u):
        queries = pl.ds(pl.multiple_of(g * GQ, GQ), GQ)
        keys = pl.ds(pl.multiple_of(u * UK, UK), UK)
        a, b = kh[keys, :], qh[queries, :]
        s = lax.dot_general(a, b, NT, preferred_element_type=F32)
        s += lax.dot_general(kl[keys, :], b, NT, preferred_element_type=F32)
        s += lax.dot_general(a, ql[queries, :], NT, preferred_element_type=F32)
        return s

    def absorb(g, u, s):
        keys = pl.ds(pl.multiple_of(u * UK, UK), UK)
        m_old = m_ref[g]
        m_new = jnp.maximum(m_old, jnp.max(s, axis=0, keepdims=True))
        shrink = jnp.exp2(m_old - m_new)
        p = jnp.exp2(s - m_new)
        m_ref[g] = m_new
        l_ref[g] = l_ref[g] * shrink + jnp.sum(p, axis=0, keepdims=True)
        high = p.astype(BF16)
        low = (p - high.astype(F32)).astype(BF16)
        v = vt[:, keys]
        o = lax.dot_general(v, high, NN, preferred_element_type=F32)
        o = o[:LAB] + o[LAB:] + lax.dot_general(v[:LAB], low, NN, preferred_element_type=F32)
        acc[g] = acc[g] * shrink + o

    def exclude_self(g, u, slot):
        @pl.when((g == OWN_GROUP) & (u == 0))
        def _():
            cols = slice(OWN_COL, OWN_COL + ROWS)
            block = s_buf[slot, :ROWS, cols]
            same = lax.broadcasted_iota(jnp.int32, block.shape, 0) == lax.broadcasted_iota(jnp.int32, block.shape, 1)
            s_buf[slot, :ROWS, cols] = jnp.where(same, NEG, block)

    tiles, before, after = split_order(ORDER)
    groups, units = [t[0] for t in tiles], [t[1] for t in tiles]
    count = len(tiles)
    complete, ended = {}, []
    for step in sorted(after):
        ended += HALVES[8 * after[step]:8 * after[step] + 8]
        complete[after[step]] = [
            slot for slot, block in enumerate(BLOCKS)
            if slot != OWN and block not in ADDED and all((*block, h) in ended for h in range(2)) and all(slot not in c for c in complete.values())
        ]

    def when_step(j, parity, table, act):
        for step in range(parity, count - 2, 2):
            if table(step):
                @pl.when(j == step)
                def _(step=step):
                    act(step)

    def act_before(step):
        for item in before[step + 1]:
            event(item)

    for item in before[0]:
        event(item)
    s_buf[0] = scores(groups[0], units[0])
    exclude_self(groups[0], units[0], 0)

    def body(i, carry):
        g, u, g_next, u_next = carry
        for parity in range(2):
            j = 2 * i + parity
            when_step(j, parity, lambda step: before[step + 1], act_before)
            following = scores(g_next, u_next)
            absorb(g, u, s_buf[parity])
            s_buf[1 - parity] = following
            exclude_self(g_next, u_next, 1 - parity)
            when_step(j, parity, lambda step: step in after, lambda step: finish(after[step]))
            g, u, g_next, u_next = g_next, u_next, pick(j + 2, groups), pick(j + 2, units)
        return g, u, g_next, u_next

    lax.fori_loop(0, (count - 2) // 2, body, tuple(jnp.int32(v) for v in tiles[0] + tiles[1]))
    for item in before[count - 1]:
        event(item)
    following = scores(groups[-1], units[-1])
    absorb(groups[-2], units[-2], s_buf[0])
    s_buf[1] = following
    if count - 2 in after:
        finish(after[count - 2])
    absorb(groups[-1], units[-1], s_buf[1])
    finish(after[count - 1])

    def combined(slot, others):
        for other in others:
            home(other).wait_recv()
        top = state[slot, LAB:LAB + 1, :]
        for other in others:
            top = jnp.maximum(top, back[other, LAB:LAB + 1, :])
        weight = jnp.exp2(state[slot, LAB:LAB + 1, :] - top)
        total = state[slot, LAB + 1:LAB + 2, :] * weight
        summed = state[slot, :LAB, :] * weight
        for other in others:
            weight = jnp.exp2(back[other, LAB:LAB + 1, :] - top)
            total += back[other, LAB + 1:LAB + 2, :] * weight
            summed += back[other, :LAB, :] * weight
        return top, total, summed

    def replace(slot, values):
        state[slot, LAB:LAB + 1, :], state[slot, LAB + 1:LAB + 2, :], state[slot, :LAB, :] = values

    for block, extra in ADDED.items():
        replace(SLOT[block], combined(SLOT[block], [SLOT[b] for b in extra]))
        home(SLOT[block]).start()
    replace(OWN, combined(OWN, [SLOT[b] for b in DIRECT]))
    top, total, summed = combined(OWN, [SLOT[b] for b in ADDED])
    out[...] = 0.1 * kf[0, :ROWS, DIM:] + 0.9 * (summed / total).T

    for n in range(10):
        for link in range(4):
            plane(link, n).wait_send()
    for r in range(NR):
        for way in range(2):
            if r > 0:
                ring(way, r).wait_send()
            across(way, r).wait_send()
    for slot in range(len(BLOCKS)):
        if slot != OWN:
            home(slot).wait_send()


def body(embeddings, labels):
    vmem = pl.BlockSpec(memory_space=pltpu.VMEM)
    return pl.pallas_call(
        kernel,
        out_shape=jax.ShapeDtypeStruct((ROWS, LAB), F32),
        in_specs=[pl.BlockSpec(memory_space=pl.ANY)] * 2,
        out_specs=vmem,
        scratch_shapes=[
            pltpu.VMEM((16, ROWS, DIM), F32),
            pltpu.VMEM((NR, RING, DIM + LAB), F32),
            pltpu.VMEM((NG * GQ, DIM), BF16),
            pltpu.VMEM((NG * GQ, DIM), BF16),
            pltpu.VMEM((NU * UK, DIM), BF16),
            pltpu.VMEM((NU * UK, DIM), BF16),
            pltpu.VMEM((2 * LAB, NU * UK), BF16),
            pltpu.VMEM((2, UK, GQ), F32),
            pltpu.VMEM((NG, LAB, GQ), F32),
            pltpu.VMEM((NG, 1, GQ), F32),
            pltpu.VMEM((NG, 1, GQ), F32),
            pltpu.VMEM((16, LAB + 8, ROWS), F32),
            pltpu.VMEM((16, LAB + 8, ROWS), F32),
            pltpu.SemaphoreType.DMA((2,)),
            pltpu.SemaphoreType.DMA((4, 10)),
            pltpu.SemaphoreType.DMA((4, 10)),
            pltpu.SemaphoreType.DMA((2, NR)),
            pltpu.SemaphoreType.DMA((2, NR)),
            pltpu.SemaphoreType.DMA((2, NR)),
            pltpu.SemaphoreType.DMA((2, NR)),
            pltpu.SemaphoreType.DMA((16,)),
            pltpu.SemaphoreType.DMA((16,)),
        ],
        compiler_params=pltpu.CompilerParams(
            collective_id=0, has_side_effects=True, vmem_limit_bytes=56 * 2**20
        ),
        name="propagate",
    )(embeddings, labels)


def solution(mesh):
    placed = P(("blk", "rep"), None)
    return jax.shard_map(body, mesh=mesh, in_specs=(placed, placed), out_specs=placed, check_vma=False)
```

```python
import math

import jax
import jax.numpy as jnp
from jax import lax
from jax.experimental import pallas as pl
from jax.experimental.pallas import tpu as pltpu
from jax.sharding import PartitionSpec as P

MESH = pl.DeviceIdType.MESH
F32, BF16 = jnp.float32, jnp.bfloat16
ROWS, DIM, LAB = 128, 768, 128
GQ, UK = 512, 512
NG, NU = 4, 4
RING, NR = 256, 8
NEG = -1e30
NT = (((1,), (1,)), ((), ()))
NN = (((1,), (0,)), ((), ()))

HALVES = [
    (1, 0, 0), (1, 0, 1), (3, 0, 0), (3, 0, 1), (0, 1, 0), (0, 1, 1), (0, 3, 0), (0, 3, 1),
    (0, 0, 0), (0, 0, 1), (2, 0, 0), (2, 0, 1), (0, 2, 0), (0, 2, 1), (1, 1, 0), (1, 1, 1),
    (3, 3, 0), (3, 3, 1), (1, 3, 0), (1, 3, 1), (3, 1, 0), (3, 1, 1), (2, 1, 0), (1, 2, 1),
    (1, 2, 0), (2, 1, 1), (3, 2, 0), (3, 2, 1), (2, 3, 0), (2, 3, 1), (2, 2, 0), (2, 2, 1),
]
BLOCKS = sorted({half[:2] for half in HALVES})
SLOT = {block: i for i, block in enumerate(BLOCKS)}
OWN = SLOT[(0, 0)]
OWN_GROUP, OWN_COL = HALVES.index((0, 0, 0)) // 8, HALVES.index((0, 0, 0)) % 8 * 64
FIRST = {(3, 3): (0, 3), (1, 3): (1, 0), (3, 1): (3, 0), (1, 2): (0, 2), (3, 2): (0, 2), (2, 1): (2, 0), (2, 3): (2, 0)}
ADDED = {(1, 0): [(1, 2)], (3, 0): [(3, 3), (3, 2)], (0, 1): [(3, 1), (2, 1)], (0, 3): [(1, 3), (2, 3)]}
DIRECT = [(2, 0), (0, 2), (2, 2), (1, 1)]
LINKS = [("x", 1), ("x", -1), ("y", 1), ("y", -1)]

ORDER = [
    ("kc", 0), ("qc", 4), ("q", 0), ("z", 1), ("kc", 1), ("q", 1), ("qc", 0), ("qc", 1), ("qc", 2), ("qc", 3),
    ("t", 0, 0), ("z", 2), ("q", 2), ("kc", 2), ("q", 3), ("qc", 5), ("qc", 6), ("z", 3), ("q", 4), ("qc", 7),
    ("kc", 3), ("t", 1, 0), ("t", 0, 1), ("z", 4), ("t", 1, 1), ("q", 5), ("kc", 4), ("q", 6), ("qc", 8), ("qc", 9),
    ("qc", 10), ("qc", 11), ("z", 5), ("t", 2, 0), ("kc", 5), ("q", 7), ("t", 2, 1), ("t", 0, 2), ("q", 8), ("z", 6),
    ("t", 1, 2), ("q", 9), ("kc", 6), ("qc", 12), ("qc", 13), ("qc", 14), ("qc", 15), ("t", 3, 0), ("t", 3, 1),
    ("z", 7), ("t", 3, 2), ("kc", 7), ("t", 3, 3), ("f", 3), ("t", 2, 2), ("t", 2, 3), ("f", 2), ("t", 1, 3),
    ("f", 1), ("t", 0, 3), ("f", 0),
]


def split_order(order):
    tiles, before, after, waiting = [], [], {}, []
    for item in order:
        if item[0] == "t":
            tiles.append((item[1], item[2]))
            before.append(waiting)
            waiting = []
        elif item[0] == "f":
            after[len(tiles) - 1] = item[1]
        else:
            waiting.append(item)
    return tiles, before, after


def pick(i, values):
    out = jnp.int32(values[0])
    for j in range(1, len(values)):
        if values[j] != values[j - 1]:
            out = jnp.where(i >= j, jnp.int32(values[j]), out)
    return out


def device(x, y, z, c):
    return ((z * 2 + y // 2) * 2 + c, x * 2 + lax.rem(y, 2))


def kernel(emb, lab, out, qf, kf, qh, ql, kh, kl, vt, s_buf, acc, m_ref, l_ref, state, back,
           in_sem, q_send, q_recv, z_send, z_recv, d_send, d_recv, b_send, b_recv):
    blk, rep = lax.axis_index("blk"), lax.axis_index("rep")
    mx, my = rep // 2, lax.rem(blk // 2, 2) * 2 + lax.rem(rep, 2)
    mz, mc = blk // 4, lax.rem(blk, 2)

    def at(dx=0, dy=0, dz=0, dc=0):
        return device(lax.rem(mx + dx % 4, 4), lax.rem(my + dy % 4, 4), lax.rem(mz + dz % 8, 8), lax.rem(mc + dc, 2))

    barrier = pltpu.get_barrier_semaphore()
    peers = [at(dx=b[0], dy=b[1]) for b in [*ADDED, *DIRECT]] + [at(dz=1), at(dz=-1), at(dc=1)]
    for peer in peers:
        pl.semaphore_signal(barrier, inc=1, device_id=peer, device_id_type=MESH)
    own = [
        pltpu.make_async_copy(emb, kf.at[0, pl.ds(0, ROWS), pl.ds(0, DIM)], in_sem.at[0]),
        pltpu.make_async_copy(lab, kf.at[0, pl.ds(0, ROWS), pl.ds(DIM, LAB)], in_sem.at[1]),
    ]
    for copy in own:
        copy.start()
    m_ref[...] = jnp.full_like(m_ref, NEG)
    l_ref[...] = jnp.zeros_like(l_ref)
    acc[...] = jnp.zeros_like(acc)
    for copy in own:
        copy.wait()
    qf[OWN] = kf[0, :ROWS, :DIM] * (math.log2(math.e) / math.sqrt(DIM))
    pl.semaphore_wait(barrier, len(peers))

    def remote(src, dst, send, recv, to):
        return pltpu.make_async_remote_copy(
            src_ref=src, dst_ref=dst, send_sem=send, recv_sem=recv, device_id=to, device_id_type=MESH
        )

    def plane(link, n):
        axis, sign = LINKS[link]
        near, far = ((0, 64), (64, 64)) if axis == "x" else ((64, 64), (0, 64))
        half = 0 if sign == 1 else 32
        near_part, far_part = (near[0] + half, 32), (far[0] + half, 32)
        along, across, part = [
            (0, 0, near), (0, 0, far), (-sign, 0, near_part), (-sign, 0, far_part),
            (0, 1, far), (0, -1, far), (0, 2, far),
            (-sign, 1, far_part), (-sign, -1, far_part), (-sign, 2, far_part),
        ][n]
        here, there = (along, across), (along - sign, across)
        step = (sign, 0)
        if axis == "y":
            here, there, step = here[::-1], there[::-1], step[::-1]
        mine = SLOT[(here[0] % 4, here[1] % 4)]
        theirs = SLOT[(there[0] % 4, there[1] % 4)]
        rows = pl.ds(part[0], part[1])
        return remote(qf.at[mine, rows], qf.at[theirs, rows], q_send.at[link, n], q_recv.at[link, n],
                      at(dx=step[0], dy=step[1]))

    def ring(way, r):
        sign = 1 if way == 0 else -1
        theirs = pl.ds(64 * way, 64)
        if r == 1:
            src = kf.at[0, pl.ds(64 * way, 64)]
        elif r == 2:
            src = kf.at[0, pl.ds(64 - 64 * way, 64)]
        else:
            src = kf.at[r - 2, theirs]
        return remote(src, kf.at[r, theirs], z_send.at[way, r], z_recv.at[way, r], at(dz=sign))

    def across(way, r):
        return remote(kf.at[r, pl.ds(64 * way, 64)], kf.at[r, pl.ds(ROWS + 64 * way, 64)],
                      d_send.at[way, r], d_recv.at[way, r], at(dc=1))

    def home(slot):
        dx, dy = FIRST.get(BLOCKS[slot], BLOCKS[slot])
        return remote(state.at[slot], back.at[slot], b_send.at[slot], b_recv.at[slot], at(dx=dx, dy=dy))

    for n in range(2):
        for link in range(4):
            plane(link, n).start()
        for way in range(2):
            ring(way, n + 1).start()
    for way in range(2):
        across(way, 0).start()

    def halves(value):
        high = value.astype(BF16)
        return high, (value - high.astype(F32)).astype(BF16)

    def convert_queries(pair):
        for i in range(2 * pair, 2 * pair + 2):
            dx, dy, half = HALVES[i]
            rows = pl.ds(i * 64, 64)
            qh[rows, :], ql[rows, :] = halves(qf[SLOT[(dx, dy)], half * 64:half * 64 + 64])

    def convert_keys(r):
        for start in range(0, RING, ROWS):
            rows = pl.ds(r * RING + start, ROWS)
            kh[rows, :], kl[rows, :] = halves(kf[r, start:start + ROWS, :DIM])
        cols = pl.ds(r * RING, RING)
        vt[:LAB, cols], vt[LAB:, cols] = halves(kf[r, :, DIM:].T)

    def event(item):
        kind, n = item
        if kind == "q":
            for link in range(4):
                plane(link, n).wait_recv()
            if n + 2 < 10:
                for link in range(4):
                    plane(link, n + 2).start()
        elif kind == "z":
            for way in range(2):
                ring(way, n).wait_recv()
                if n + 2 < NR:
                    ring(way, n + 2).start()
                across(way, n).start()
        elif kind == "kc":
            for way in range(2):
                across(way, n).wait_recv()
            convert_keys(n)
        else:
            convert_queries(n)

    def finish(g):
        for pair in range(4):
            first, second = (SLOT[HALVES[8 * g + 2 * pair + h][:2]] for h in range(2))
            cols = slice(pair * ROWS, (pair + 1) * ROWS)
            for rows, value in (
                (slice(0, LAB), acc[g, :, cols]),
                (slice(LAB, LAB + 1), m_ref[g, :, cols]),
                (slice(LAB + 1, LAB + 2), l_ref[g, :, cols]),
            ):
                if first == second:
                    state[first, rows, :] = value
                else:
                    state[first, rows, :64] = value[:, :64]
                    state[second, rows, 64:] = value[:, 64:]
        for slot in complete[g]:
            home(slot).start()

    def scores(g, u):
        queries = pl.ds(pl.multiple_of(g * GQ, GQ), GQ)
        keys = pl.ds(pl.multiple_of(u * UK, UK), UK)
        a, b = kh[keys, :], qh[queries, :]
        s = lax.dot_general(a, b, NT, preferred_element_type=F32)
        s += lax.dot_general(kl[keys, :], b, NT, preferred_element_type=F32)
        s += lax.dot_general(a, ql[queries, :], NT, preferred_element_type=F32)
        return s

    def absorb(g, u, s):
        keys = pl.ds(pl.multiple_of(u * UK, UK), UK)
        m_old = m_ref[g]
        m_new = jnp.maximum(m_old, jnp.max(s, axis=0, keepdims=True))
        shrink = jnp.exp2(m_old - m_new)
        p = jnp.exp2(s - m_new)
        m_ref[g] = m_new
        l_ref[g] = l_ref[g] * shrink + jnp.sum(p, axis=0, keepdims=True)
        high = p.astype(BF16)
        low = (p - high.astype(F32)).astype(BF16)
        v = vt[:, keys]
        o = lax.dot_general(v, high, NN, preferred_element_type=F32)
        o = o[:LAB] + o[LAB:] + lax.dot_general(v[:LAB], low, NN, preferred_element_type=F32)
        acc[g] = acc[g] * shrink + o

    def exclude_self(g, u, slot):
        @pl.when((g == OWN_GROUP) & (u == 0))
        def _():
            cols = slice(OWN_COL, OWN_COL + ROWS)
            block = s_buf[slot, :ROWS, cols]
            same = lax.broadcasted_iota(jnp.int32, block.shape, 0) == lax.broadcasted_iota(jnp.int32, block.shape, 1)
            s_buf[slot, :ROWS, cols] = jnp.where(same, NEG, block)

    tiles, before, after = split_order(ORDER)
    groups, units = [t[0] for t in tiles], [t[1] for t in tiles]
    count = len(tiles)
    complete, ended = {}, []
    for step in sorted(after):
        ended += HALVES[8 * after[step]:8 * after[step] + 8]
        complete[after[step]] = [
            slot for slot, block in enumerate(BLOCKS)
            if slot != OWN and block not in ADDED and all((*block, h) in ended for h in range(2)) and all(slot not in c for c in complete.values())
        ]

    def when_step(j, parity, table, act):
        for step in range(parity, count - 2, 2):
            if table(step):
                @pl.when(j == step)
                def _(step=step):
                    act(step)

    def act_before(step):
        for item in before[step + 1]:
            event(item)

    for item in before[0]:
        event(item)
    s_buf[0] = scores(groups[0], units[0])
    exclude_self(groups[0], units[0], 0)

    def body(i, carry):
        g, u, g_next, u_next = carry
        for parity in range(2):
            j = 2 * i + parity
            when_step(j, parity, lambda step: before[step + 1], act_before)
            following = scores(g_next, u_next)
            absorb(g, u, s_buf[parity])
            s_buf[1 - parity] = following
            exclude_self(g_next, u_next, 1 - parity)
            when_step(j, parity, lambda step: step in after, lambda step: finish(after[step]))
            g, u, g_next, u_next = g_next, u_next, pick(j + 2, groups), pick(j + 2, units)
        return g, u, g_next, u_next

    lax.fori_loop(0, (count - 2) // 2, body, tuple(jnp.int32(v) for v in tiles[0] + tiles[1]))
    for item in before[count - 1]:
        event(item)
    following = scores(groups[-1], units[-1])
    absorb(groups[-2], units[-2], s_buf[0])
    s_buf[1] = following
    if count - 2 in after:
        finish(after[count - 2])
    absorb(groups[-1], units[-1], s_buf[1])
    finish(after[count - 1])

    def combined(slot, others):
        for other in others:
            home(other).wait_recv()
        top = state[slot, LAB:LAB + 1, :]
        for other in others:
            top = jnp.maximum(top, back[other, LAB:LAB + 1, :])
        weight = jnp.exp2(state[slot, LAB:LAB + 1, :] - top)
        total = state[slot, LAB + 1:LAB + 2, :] * weight
        summed = state[slot, :LAB, :] * weight
        for other in others:
            weight = jnp.exp2(back[other, LAB:LAB + 1, :] - top)
            total += back[other, LAB + 1:LAB + 2, :] * weight
            summed += back[other, :LAB, :] * weight
        return top, total, summed

    def replace(slot, values):
        state[slot, LAB:LAB + 1, :], state[slot, LAB + 1:LAB + 2, :], state[slot, :LAB, :] = values

    for block, extra in ADDED.items():
        replace(SLOT[block], combined(SLOT[block], [SLOT[b] for b in extra]))
        home(SLOT[block]).start()
    replace(OWN, combined(OWN, [SLOT[b] for b in DIRECT]))
    top, total, summed = combined(OWN, [SLOT[b] for b in ADDED])
    out[...] = 0.1 * kf[0, :ROWS, DIM:] + 0.9 * (summed / total).T

    for n in range(10):
        for link in range(4):
            plane(link, n).wait_send()
    for r in range(NR):
        for way in range(2):
            if r > 0:
                ring(way, r).wait_send()
            across(way, r).wait_send()
    for slot in range(len(BLOCKS)):
        if slot != OWN:
            home(slot).wait_send()


def body(embeddings, labels):
    vmem = pl.BlockSpec(memory_space=pltpu.VMEM)
    return pl.pallas_call(
        kernel,
        out_shape=jax.ShapeDtypeStruct((ROWS, LAB), F32),
        in_specs=[pl.BlockSpec(memory_space=pl.ANY)] * 2,
        out_specs=vmem,
        scratch_shapes=[
            pltpu.VMEM((16, ROWS, DIM), F32),
            pltpu.VMEM((NR, RING, DIM + LAB), F32),
            pltpu.VMEM((NG * GQ, DIM), BF16),
            pltpu.VMEM((NG * GQ, DIM), BF16),
            pltpu.VMEM((NU * UK, DIM), BF16),
            pltpu.VMEM((NU * UK, DIM), BF16),
            pltpu.VMEM((2 * LAB, NU * UK), BF16),
            pltpu.VMEM((2, UK, GQ), F32),
            pltpu.VMEM((NG, LAB, GQ), F32),
            pltpu.VMEM((NG, 1, GQ), F32),
            pltpu.VMEM((NG, 1, GQ), F32),
            pltpu.VMEM((16, LAB + 8, ROWS), F32),
            pltpu.VMEM((16, LAB + 8, ROWS), F32),
            pltpu.SemaphoreType.DMA((2,)),
            pltpu.SemaphoreType.DMA((4, 10)),
            pltpu.SemaphoreType.DMA((4, 10)),
            pltpu.SemaphoreType.DMA((2, NR)),
            pltpu.SemaphoreType.DMA((2, NR)),
            pltpu.SemaphoreType.DMA((2, NR)),
            pltpu.SemaphoreType.DMA((2, NR)),
            pltpu.SemaphoreType.DMA((16,)),
            pltpu.SemaphoreType.DMA((16,)),
        ],
        compiler_params=pltpu.CompilerParams(
            collective_id=0, has_side_effects=True, vmem_limit_bytes=56 * 2**20
        ),
        name="propagate",
    )(embeddings, labels)


def solution(mesh):
    placed = P(("blk", "rep"), None)
    return jax.shard_map(body, mesh=mesh, in_specs=(placed, placed), out_specs=placed, check_vma=False)
```

```python
import math

import jax
import jax.numpy as jnp
from jax import lax
from jax.experimental import pallas as pl
from jax.experimental.pallas import tpu as pltpu
from jax.sharding import PartitionSpec as P

MESH = pl.DeviceIdType.MESH
F32, BF16 = jnp.float32, jnp.bfloat16
ROWS, DIM, LAB = 128, 768, 128
GQ, UK = 512, 512
NG, NU = 4, 4
RING, NR = 256, 8
NEG = -1e30
NT = (((1,), (1,)), ((), ()))
NN = (((1,), (0,)), ((), ()))

HALVES = [
    (1, 0, 0), (1, 0, 1), (3, 0, 0), (3, 0, 1), (0, 1, 0), (0, 1, 1), (0, 3, 0), (0, 3, 1),
    (0, 0, 0), (0, 0, 1), (2, 0, 0), (2, 0, 1), (0, 2, 0), (0, 2, 1), (1, 1, 0), (1, 1, 1),
    (3, 3, 0), (3, 3, 1), (1, 3, 0), (1, 3, 1), (3, 1, 0), (3, 1, 1), (2, 1, 0), (1, 2, 1),
    (1, 2, 0), (2, 1, 1), (3, 2, 0), (3, 2, 1), (2, 3, 0), (2, 3, 1), (2, 2, 0), (2, 2, 1),
]
BLOCKS = sorted({half[:2] for half in HALVES})
SLOT = {block: i for i, block in enumerate(BLOCKS)}
OWN = SLOT[(0, 0)]
OWN_GROUP, OWN_COL = HALVES.index((0, 0, 0)) // 8, HALVES.index((0, 0, 0)) % 8 * 64
FIRST = {(3, 3): (0, 3), (1, 3): (1, 0), (3, 1): (3, 0), (1, 2): (0, 2), (3, 2): (0, 2), (2, 1): (2, 0), (2, 3): (2, 0)}
ADDED = {(1, 0): [(1, 2)], (3, 0): [(3, 3), (3, 2)], (0, 1): [(3, 1), (2, 1)], (0, 3): [(1, 3), (2, 3)]}
DIRECT = [(2, 0), (0, 2), (2, 2), (1, 1)]
LINKS = [("x", 1), ("x", -1), ("y", 1), ("y", -1)]

ORDER = [
    ("kc", 0), ("qc", 4), ("q", 0), ("z", 1), ("kc", 1), ("q", 1), ("qc", 0), ("qc", 1), ("qc", 2), ("qc", 3),
    ("t", 0, 0), ("z", 2), ("q", 2), ("kc", 2), ("q", 3), ("qc", 5), ("qc", 6), ("z", 3), ("q", 4), ("qc", 7),
    ("kc", 3), ("t", 1, 0), ("t", 0, 1), ("z", 4), ("t", 1, 1), ("q", 5), ("kc", 4), ("q", 6), ("qc", 8), ("qc", 9),
    ("qc", 10), ("qc", 11), ("z", 5), ("t", 2, 0), ("kc", 5), ("q", 7), ("t", 2, 1), ("t", 0, 2), ("z", 6),
    ("t", 1, 2), ("kc", 6), ("qc", 12), ("q", 8), ("qc", 13), ("qc", 14), ("q", 9), ("qc", 15), ("t", 3, 0),
    ("t", 3, 1), ("z", 7), ("t", 3, 2), ("kc", 7), ("t", 3, 3), ("f", 3), ("t", 2, 2), ("t", 2, 3), ("f", 2),
    ("t", 1, 3), ("f", 1), ("t", 0, 3), ("f", 0),
]


def split_order(order):
    tiles, before, after, waiting = [], [], {}, []
    for item in order:
        if item[0] == "t":
            tiles.append((item[1], item[2]))
            before.append(waiting)
            waiting = []
        elif item[0] == "f":
            after[len(tiles) - 1] = item[1]
        else:
            waiting.append(item)
    return tiles, before, after


def pick(i, values):
    out = jnp.int32(values[0])
    for j in range(1, len(values)):
        if values[j] != values[j - 1]:
            out = jnp.where(i >= j, jnp.int32(values[j]), out)
    return out


def device(x, y, z, c):
    return ((z * 2 + y // 2) * 2 + c, x * 2 + lax.rem(y, 2))


def kernel(emb, lab, out, qf, kf, qh, ql, kh, kl, vt, s_buf, acc, m_ref, l_ref, state, back,
           in_sem, q_send, q_recv, z_send, z_recv, d_send, d_recv, b_send, b_recv):
    blk, rep = lax.axis_index("blk"), lax.axis_index("rep")
    mx, my = rep // 2, lax.rem(blk // 2, 2) * 2 + lax.rem(rep, 2)
    mz, mc = blk // 4, lax.rem(blk, 2)

    def at(dx=0, dy=0, dz=0, dc=0):
        return device(lax.rem(mx + dx % 4, 4), lax.rem(my + dy % 4, 4), lax.rem(mz + dz % 8, 8), lax.rem(mc + dc, 2))

    barrier = pltpu.get_barrier_semaphore()
    peers = [at(dx=b[0], dy=b[1]) for b in [*ADDED, *DIRECT]] + [at(dz=1), at(dz=-1), at(dc=1)]
    for peer in peers:
        pl.semaphore_signal(barrier, inc=1, device_id=peer, device_id_type=MESH)
    own = [
        pltpu.make_async_copy(emb, kf.at[0, pl.ds(0, ROWS), pl.ds(0, DIM)], in_sem.at[0]),
        pltpu.make_async_copy(lab, kf.at[0, pl.ds(0, ROWS), pl.ds(DIM, LAB)], in_sem.at[1]),
    ]
    for copy in own:
        copy.start()
    m_ref[...] = jnp.full_like(m_ref, NEG)
    l_ref[...] = jnp.zeros_like(l_ref)
    acc[...] = jnp.zeros_like(acc)
    for copy in own:
        copy.wait()
    qf[OWN] = kf[0, :ROWS, :DIM] * (math.log2(math.e) / math.sqrt(DIM))
    pl.semaphore_wait(barrier, len(peers))

    def remote(src, dst, send, recv, to):
        return pltpu.make_async_remote_copy(
            src_ref=src, dst_ref=dst, send_sem=send, recv_sem=recv, device_id=to, device_id_type=MESH
        )

    def plane(link, n):
        axis, sign = LINKS[link]
        near, far = ((0, 64), (64, 64)) if axis == "x" else ((64, 64), (0, 64))
        half = 0 if sign == 1 else 32
        near_part, far_part = (near[0] + half, 32), (far[0] + half, 32)
        along, across, part = [
            (0, 0, near), (0, 0, far), (-sign, 0, near_part), (-sign, 0, far_part),
            (0, 1, far), (0, -1, far), (0, 2, far),
            (-sign, 1, far_part), (-sign, -1, far_part), (-sign, 2, far_part),
        ][n]
        here, there = (along, across), (along - sign, across)
        step = (sign, 0)
        if axis == "y":
            here, there, step = here[::-1], there[::-1], step[::-1]
        mine = SLOT[(here[0] % 4, here[1] % 4)]
        theirs = SLOT[(there[0] % 4, there[1] % 4)]
        rows = pl.ds(part[0], part[1])
        return remote(qf.at[mine, rows], qf.at[theirs, rows], q_send.at[link, n], q_recv.at[link, n],
                      at(dx=step[0], dy=step[1]))

    def ring(way, r):
        sign = 1 if way == 0 else -1
        theirs = pl.ds(64 * way, 64)
        if r == 1:
            src = kf.at[0, pl.ds(64 * way, 64)]
        elif r == 2:
            src = kf.at[0, pl.ds(64 - 64 * way, 64)]
        else:
            src = kf.at[r - 2, theirs]
        return remote(src, kf.at[r, theirs], z_send.at[way, r], z_recv.at[way, r], at(dz=sign))

    def across(way, r):
        return remote(kf.at[r, pl.ds(64 * way, 64)], kf.at[r, pl.ds(ROWS + 64 * way, 64)],
                      d_send.at[way, r], d_recv.at[way, r], at(dc=1))

    def home(slot):
        dx, dy = FIRST.get(BLOCKS[slot], BLOCKS[slot])
        return remote(state.at[slot], back.at[slot], b_send.at[slot], b_recv.at[slot], at(dx=dx, dy=dy))

    for n in range(2):
        for link in range(4):
            plane(link, n).start()
        for way in range(2):
            ring(way, n + 1).start()
    for way in range(2):
        across(way, 0).start()

    def halves(value):
        high = value.astype(BF16)
        return high, (value - high.astype(F32)).astype(BF16)

    def convert_queries(pair):
        for i in range(2 * pair, 2 * pair + 2):
            dx, dy, half = HALVES[i]
            rows = pl.ds(i * 64, 64)
            qh[rows, :], ql[rows, :] = halves(qf[SLOT[(dx, dy)], half * 64:half * 64 + 64])

    def convert_keys(r):
        for start in range(0, RING, ROWS):
            rows = pl.ds(r * RING + start, ROWS)
            kh[rows, :], kl[rows, :] = halves(kf[r, start:start + ROWS, :DIM])
        cols = pl.ds(r * RING, RING)
        vt[:LAB, cols], vt[LAB:, cols] = halves(kf[r, :, DIM:].T)

    def event(item):
        kind, n = item
        if kind == "q":
            for link in range(4):
                plane(link, n).wait_recv()
            if n + 2 < 10:
                for link in range(4):
                    plane(link, n + 2).start()
        elif kind == "z":
            for way in range(2):
                ring(way, n).wait_recv()
                if n + 2 < NR:
                    ring(way, n + 2).start()
                across(way, n).start()
        elif kind == "kc":
            for way in range(2):
                across(way, n).wait_recv()
            convert_keys(n)
        else:
            convert_queries(n)

    def finish(g):
        for pair in range(4):
            first, second = (SLOT[HALVES[8 * g + 2 * pair + h][:2]] for h in range(2))
            cols = slice(pair * ROWS, (pair + 1) * ROWS)
            for rows, value in (
                (slice(0, LAB), acc[g, :, cols]),
                (slice(LAB, LAB + 1), m_ref[g, :, cols]),
                (slice(LAB + 1, LAB + 2), l_ref[g, :, cols]),
            ):
                if first == second:
                    state[first, rows, :] = value
                else:
                    state[first, rows, :64] = value[:, :64]
                    state[second, rows, 64:] = value[:, 64:]
        for slot in complete[g]:
            home(slot).start()

    def scores(g, u):
        queries = pl.ds(pl.multiple_of(g * GQ, GQ), GQ)
        keys = pl.ds(pl.multiple_of(u * UK, UK), UK)
        a, b = kh[keys, :], qh[queries, :]
        s = lax.dot_general(a, b, NT, preferred_element_type=F32)
        s += lax.dot_general(kl[keys, :], b, NT, preferred_element_type=F32)
        s += lax.dot_general(a, ql[queries, :], NT, preferred_element_type=F32)
        return s

    def absorb(g, u, s):
        keys = pl.ds(pl.multiple_of(u * UK, UK), UK)
        m_old = m_ref[g]
        m_new = jnp.maximum(m_old, jnp.max(s, axis=0, keepdims=True))
        shrink = jnp.exp2(m_old - m_new)
        p = jnp.exp2(s - m_new)
        m_ref[g] = m_new
        l_ref[g] = l_ref[g] * shrink + jnp.sum(p, axis=0, keepdims=True)
        high = p.astype(BF16)
        low = (p - high.astype(F32)).astype(BF16)
        v = vt[:, keys]
        o = lax.dot_general(v, high, NN, preferred_element_type=F32)
        o = o[:LAB] + o[LAB:] + lax.dot_general(v[:LAB], low, NN, preferred_element_type=F32)
        acc[g] = acc[g] * shrink + o

    def exclude_self(g, u, slot):
        @pl.when((g == OWN_GROUP) & (u == 0))
        def _():
            cols = slice(OWN_COL, OWN_COL + ROWS)
            block = s_buf[slot, :ROWS, cols]
            same = lax.broadcasted_iota(jnp.int32, block.shape, 0) == lax.broadcasted_iota(jnp.int32, block.shape, 1)
            s_buf[slot, :ROWS, cols] = jnp.where(same, NEG, block)

    tiles, before, after = split_order(ORDER)
    groups, units = [t[0] for t in tiles], [t[1] for t in tiles]
    count = len(tiles)
    complete, ended = {}, []
    for step in sorted(after):
        ended += HALVES[8 * after[step]:8 * after[step] + 8]
        complete[after[step]] = [
            slot for slot, block in enumerate(BLOCKS)
            if slot != OWN and block not in ADDED and all((*block, h) in ended for h in range(2)) and all(slot not in c for c in complete.values())
        ]

    def when_step(j, parity, table, act):
        for step in range(parity, count - 2, 2):
            if table(step):
                @pl.when(j == step)
                def _(step=step):
                    act(step)

    def act_before(step):
        for item in before[step + 1]:
            event(item)

    for item in before[0]:
        event(item)
    s_buf[0] = scores(groups[0], units[0])
    exclude_self(groups[0], units[0], 0)

    def body(i, carry):
        g, u, g_next, u_next = carry
        for parity in range(2):
            j = 2 * i + parity
            when_step(j, parity, lambda step: before[step + 1], act_before)
            following = scores(g_next, u_next)
            absorb(g, u, s_buf[parity])
            s_buf[1 - parity] = following
            exclude_self(g_next, u_next, 1 - parity)
            when_step(j, parity, lambda step: step in after, lambda step: finish(after[step]))
            g, u, g_next, u_next = g_next, u_next, pick(j + 2, groups), pick(j + 2, units)
        return g, u, g_next, u_next

    lax.fori_loop(0, (count - 2) // 2, body, tuple(jnp.int32(v) for v in tiles[0] + tiles[1]))
    for item in before[count - 1]:
        event(item)
    following = scores(groups[-1], units[-1])
    absorb(groups[-2], units[-2], s_buf[0])
    s_buf[1] = following
    if count - 2 in after:
        finish(after[count - 2])
    absorb(groups[-1], units[-1], s_buf[1])
    finish(after[count - 1])

    def combined(slot, others):
        for other in others:
            home(other).wait_recv()
        top = state[slot, LAB:LAB + 1, :]
        for other in others:
            top = jnp.maximum(top, back[other, LAB:LAB + 1, :])
        weight = jnp.exp2(state[slot, LAB:LAB + 1, :] - top)
        total = state[slot, LAB + 1:LAB + 2, :] * weight
        summed = state[slot, :LAB, :] * weight
        for other in others:
            weight = jnp.exp2(back[other, LAB:LAB + 1, :] - top)
            total += back[other, LAB + 1:LAB + 2, :] * weight
            summed += back[other, :LAB, :] * weight
        return top, total, summed

    def replace(slot, values):
        state[slot, LAB:LAB + 1, :], state[slot, LAB + 1:LAB + 2, :], state[slot, :LAB, :] = values

    for block, extra in ADDED.items():
        replace(SLOT[block], combined(SLOT[block], [SLOT[b] for b in extra]))
        home(SLOT[block]).start()
    replace(OWN, combined(OWN, [SLOT[b] for b in DIRECT]))
    top, total, summed = combined(OWN, [SLOT[b] for b in ADDED])
    out[...] = 0.1 * kf[0, :ROWS, DIM:] + 0.9 * (summed / total).T

    for n in range(10):
        for link in range(4):
            plane(link, n).wait_send()
    for r in range(NR):
        for way in range(2):
            if r > 0:
                ring(way, r).wait_send()
            across(way, r).wait_send()
    for slot in range(len(BLOCKS)):
        if slot != OWN:
            home(slot).wait_send()


def body(embeddings, labels):
    vmem = pl.BlockSpec(memory_space=pltpu.VMEM)
    return pl.pallas_call(
        kernel,
        out_shape=jax.ShapeDtypeStruct((ROWS, LAB), F32),
        in_specs=[pl.BlockSpec(memory_space=pl.ANY)] * 2,
        out_specs=vmem,
        scratch_shapes=[
            pltpu.VMEM((16, ROWS, DIM), F32),
            pltpu.VMEM((NR, RING, DIM + LAB), F32),
            pltpu.VMEM((NG * GQ, DIM), BF16),
            pltpu.VMEM((NG * GQ, DIM), BF16),
            pltpu.VMEM((NU * UK, DIM), BF16),
            pltpu.VMEM((NU * UK, DIM), BF16),
            pltpu.VMEM((2 * LAB, NU * UK), BF16),
            pltpu.VMEM((2, UK, GQ), F32),
            pltpu.VMEM((NG, LAB, GQ), F32),
            pltpu.VMEM((NG, 1, GQ), F32),
            pltpu.VMEM((NG, 1, GQ), F32),
            pltpu.VMEM((16, LAB + 8, ROWS), F32),
            pltpu.VMEM((16, LAB + 8, ROWS), F32),
            pltpu.SemaphoreType.DMA((2,)),
            pltpu.SemaphoreType.DMA((4, 10)),
            pltpu.SemaphoreType.DMA((4, 10)),
            pltpu.SemaphoreType.DMA((2, NR)),
            pltpu.SemaphoreType.DMA((2, NR)),
            pltpu.SemaphoreType.DMA((2, NR)),
            pltpu.SemaphoreType.DMA((2, NR)),
            pltpu.SemaphoreType.DMA((16,)),
            pltpu.SemaphoreType.DMA((16,)),
        ],
        compiler_params=pltpu.CompilerParams(
            collective_id=0, has_side_effects=True, vmem_limit_bytes=56 * 2**20
        ),
        name="propagate",
    )(embeddings, labels)


def solution(mesh):
    placed = P(("blk", "rep"), None)
    return jax.shard_map(body, mesh=mesh, in_specs=(placed, placed), out_specs=placed, check_vma=False)
```
